256 devices in a mesh: dp: 16 (over y_hi, x, core), tensor: 16 (over y_lo, z).
Axes of the slice: x: 4, y: 4 (y_hi: 2, y_lo: 2; y = y_hi * 2 + y_lo), z: 8, core: 2. Of those that a mesh axis runs over, the one named last changes fastest.
Arguments:
- resid: bfloat16 [2048, 8192], P('dp', 'tensor'), may hold values from -6 to 6
- norm_gain: bfloat16 [8192], P('tensor'), may hold values from 0.099609375 to 1.8984375
- cotangent: bfloat16 [2048, 8192], P('dp'), may hold values from -0.13183594 to 0.13183594
- w_gate: bfloat16 [8192, 14336], P('dp', 'tensor'), may hold values from -0.0625 to 0.0625
- w_up: bfloat16 [8192, 14336], P('dp', 'tensor'), may hold values from -0.0625 to 0.0625
- tan_gate: bfloat16 [8192, 14336], P('dp', 'tensor'), may hold values from -0.0625 to 0.0625
- tan_up: bfloat16 [8192, 14336], P('dp', 'tensor'), may hold values from -0.0625 to 0.0625
- w_down: bfloat16 [14336, 8192], P('tensor', 'dp'), may hold values from -0.0625 to 0.0625
Outputs:
- hvp_gate: float32 [8192, 14336], P('dp', 'tensor')
- hvp_up: float32 [8192, 14336], P('dp', 'tensor')
The draws below stay inside these ranges and needn't reach their ends.
All inputs are finite; a program needn't handle non-finite values.
Results may differ from the reference program's by a relative error of at most 0.028.
Values may be sent and summed in bfloat16 or wider, within the bound.
No kernel may reach another device: no remote copies, remote signals or barrier semaphores. Data moves between devices by JAX's collectives and lax.ppermute only.
A program may use at most 192 MiB of HBM per device.

```python
import jax
import jax.numpy as jnp
from jax import lax

D = 8192
FF = 14336
TOKENS = 2048
N_DP = 16


def steps_of(stream_key, shape, pieces, low, largest):
    gain, own = 1.0, jax.random.fold_in(stream_key, 6)
    for position, blocks in pieces:
        draws = jnp.exp(jax.random.uniform(jax.random.fold_in(own, position), (blocks,), jnp.float32, low / len(pieces), largest / len(pieces)))
        gain = gain * jnp.repeat(draws, shape[position] // blocks).reshape([-1 if axis == position else 1 for axis in range(len(shape))])
    return gain


def scatter_about(key, dims, deviation, limit, cuts=(), held_as=jnp.bfloat16):
    values = jax.random.normal(key, dims, jnp.float32) * deviation
    if len(cuts) > 0:
        values = steps_of(key, dims, cuts, -0.22, 0.18) * values
    return jnp.clip(values, min=-limit, max=limit).astype(held_as)


def setup_inputs(seed: int = 0) -> dict:
    keys = jax.random.split(jax.random.key(seed), 9)
    resid = scatter_about(keys[0], (TOKENS, D), 1.0, 6.0, ((0, 16), (1, 16)))
    norm_gain = jnp.clip(1.0 + 0.18 * jax.random.normal(keys[1], (D,), jnp.float32), 0.099609375, 1.8984375).astype(jnp.bfloat16)
    cotangent = scatter_about(keys[2], (TOKENS, D), (TOKENS ** -0.5), 0.13183594, ((0, 16),))
    w_gate = scatter_about(keys[3], (D, FF), D ** -0.5, 0.0625, ((0, 16), (1, 16)))
    w_up = scatter_about(keys[4], (D, FF), D ** -0.5, 0.0625, ((0, 16), (1, 16)))
    tan_gate = scatter_about(keys[5], (D, FF), D ** -0.5, 0.0625, ((0, 16), (1, 16)))
    tan_up = scatter_about(keys[6], (D, FF), D ** -0.5, 0.0625, ((0, 16), (1, 16)))
    w_down = scatter_about(keys[7], (FF, D), D ** -0.5, 0.0625, ((0, 16), (1, 16)))
    return {"resid": resid, "norm_gain": norm_gain, "cotangent": cotangent, "w_gate": w_gate, "w_up": w_up, "tan_gate": tan_gate, "tan_up": tan_up, "w_down": w_down}


epsilon = 1e-05

def block_products(normed, cotangent, w_gate, w_up, tan_gate, tan_up, w_down):
    block_width = D // N_DP
    zeros_tuple = tuple((jnp.zeros((TOKENS, FF), jnp.float32) for _ in range(5)))

    def step(running, block_index):
        offset = (block_index * block_width).astype(jnp.int32)
        feature_rows = lax.dynamic_slice_in_dim(normed, offset, block_width, 1)
        cot_rows = lax.dynamic_slice_in_dim(cotangent, offset, block_width, 1)
        products = [jnp.dot(feature_rows, lax.dynamic_slice_in_dim(weight, offset, block_width, 0), preferred_element_type=jnp.float32) for weight in (w_gate, w_up, tan_gate, tan_up)]
        down_cols = lax.dynamic_slice_in_dim(w_down, offset, block_width, 1)
        products.append(lax.dot_general(cot_rows, down_cols, (((1,), (1,)), ((), ())), preferred_element_type=jnp.float32))
        rounded = [lax.optimization_barrier(item.astype(jnp.bfloat16)).astype(jnp.float32) for item in products]
        return (tuple((total + item for total, item in zip(running, rounded))), None)
    result, _ = lax.scan(step, zeros_tuple, jnp.arange(N_DP, dtype=jnp.int32))
    return result

def reference(resid, norm_gain, cotangent, w_gate, w_up, tan_gate, tan_up, w_down):
    widened = resid.astype(jnp.float32)
    mean_square = lax.optimization_barrier(jnp.mean(widened * widened, axis=1, keepdims=True))
    normed = (widened * lax.rsqrt(mean_square + epsilon) * norm_gain.astype(jnp.float32)).astype(jnp.bfloat16)
    gate, up_proj, gate_dot, up_dot, back = block_products(normed, cotangent, w_gate, w_up, tan_gate, tan_up, w_down)
    sigmoid = jax.nn.sigmoid(gate)
    first = sigmoid * (1.0 + gate * (1.0 - sigmoid))
    second = sigmoid * (1.0 - sigmoid) * (2.0 + gate * (1.0 - 2.0 * sigmoid))
    gate_adj = (back * (up_dot * first + up_proj * second * gate_dot)).astype(jnp.bfloat16)
    up_adj = (back * first * gate_dot).astype(jnp.bfloat16)
    hvp_gate = jnp.dot(normed.T, gate_adj, preferred_element_type=jnp.float32)
    hvp_up = jnp.dot(normed.T, up_adj, preferred_element_type=jnp.float32)
    return (hvp_gate, hvp_up)
```

```python
import jax
import jax.numpy as jnp
from jax import lax
from jax.sharding import PartitionSpec as P

epsilon = 1e-05
BF = jnp.bfloat16
F32 = jnp.float32

ORDER = ((1, 0), (2, 0), (1, 1), (2, 1), (0, 1), (3, 1), (0, 0), (3, 0))


def split(dp):
    return dp // 8, dp // 2 % 4, dp % 2


def join(yh, x, c):
    return yh * 8 + x * 2 + c


def first_partner(dp):
    yh, x, c = split(dp)
    return join(yh, x ^ (3 if c else 1), c)


def second_partner(dp):
    yh, x, c = split(dp)
    return join(yh, x ^ (1 if c else 3), c)


PERM_P1 = [(d, first_partner(d)) for d in range(16)]
PERM_P2 = [(d, second_partner(d)) for d in range(16)]
PERM_Y = [(d, d ^ 8) for d in range(16)]
PERM_C = [(d, d ^ 1) for d in range(16)]
PERM_YL = [(t, t ^ 8) for t in range(16)]
PERM_UP = [(t, t // 8 * 8 + (t % 8 + 1) % 8) for t in range(16)]
PERM_DOWN = [(t, t // 8 * 8 + (t % 8 + 7) % 8) for t in range(16)]


def transposed():
    pairs = []
    for dp in range(16):
        yh, x, c = split(dp)
        for t in range(16):
            owner = t // 2
            to_yh, to_x = owner // 4, owner % 4
            step = x ^ to_x
            q = (-step) % 4 if c else step
            position = ORDER.index((q, yh ^ to_yh))
            half = (t % 2) ^ c
            pairs.append((dp * 16 + t, join(to_yh, to_x, c) * 16 + half * 8 + position))
    return pairs


PERM_T = transposed()


def dot(a, b):
    return jnp.dot(a, b, preferred_element_type=F32)


def dot_t(a, b):
    return lax.dot_general(a, b, (((1,), (1,)), ((), ())), preferred_element_type=F32)


def dot_0(a, b):
    return lax.dot_general(a, b, (((0,), (0,)), ((), ())), preferred_element_type=F32)


def go(a, perm):
    return lax.ppermute(a, "dp", perm)


def sum_x_first(rows, weight, mul):
    near = go(mul(rows[:512], weight).astype(BF), PERM_P1)
    kept = mul(rows[512:], weight)
    far_s = kept[:256] + near[256:].astype(F32)
    own_s = kept[256:] + near[:256].astype(F32)
    second = go(jnp.concatenate([far_s[128:], own_s[128:]], axis=0).astype(BF), PERM_P2)
    last = go((far_s[:128] + second[:128].astype(F32)).astype(BF), PERM_Y)
    return own_s[:128] + second[128:].astype(F32) + last.astype(F32)


def sum_y_first(rows, weight, mul):
    near = go(mul(rows[256:768], weight).astype(BF), PERM_Y)
    second = go((mul(rows[:256], weight) + near[:256].astype(F32)).astype(BF), PERM_P1)
    kept = mul(rows[768:], weight) + near[256:].astype(F32) + second.astype(F32)
    last = go(kept[128:].astype(BF), PERM_P2)
    return kept[:128] + last.astype(F32)


def spread_y_first(own):
    pair = jnp.concatenate([go(own, PERM_Y), own], axis=0)
    second = go(pair, PERM_P2)
    kept = jnp.concatenate([pair[:128], second[:128], pair[128:], second[128:]], axis=0)
    last = go(kept, PERM_P1)
    return jnp.concatenate([last[256:], last[:256], kept], axis=0)


def spread_x_first(own):
    pair = jnp.concatenate([own, go(own, PERM_P2)], axis=0)
    second = go(pair, PERM_P1)
    last = go(jnp.concatenate([second, pair], axis=0), PERM_Y)
    return jnp.concatenate([second, last, pair], axis=0)


def ring_gather(own, place):
    rows = own.shape[0]
    half = rows // 2
    parts = [(0, own)]
    up = down = own
    for step in range(1, 4):
        up = lax.ppermute(up, "tensor", PERM_UP)
        down = lax.ppermute(down, "tensor", PERM_DOWN)
        parts += [(-step, up), (step, down)]
    top = lax.ppermute(up[:half], "tensor", PERM_UP)
    bottom = lax.ppermute(down[half:], "tensor", PERM_DOWN)
    parts.append((4, jnp.concatenate([top, bottom], axis=0)))
    out = jnp.zeros((8 * rows, own.shape[1]), own.dtype)
    for offset, part in parts:
        out = lax.dynamic_update_slice(out, part, ((place + offset + 8) % 8 * rows, 0))
    return out


def on_device(resid, norm_gain, cotangent, w_gate, w_up, tan_gate, tan_up, w_down):
    dp, tensor = lax.axis_index("dp"), lax.axis_index("tensor")
    yh, x, core = dp // 8, dp // 2 % 4, dp % 2
    hidden = w_gate.shape[1]

    wide = resid.astype(F32)
    scaled = (wide * norm_gain.astype(F32)[None, :]).astype(BF)
    moved = lax.ppermute(scaled, ("dp", "tensor"), PERM_T)

    blocks = cotangent.reshape(128, 8, 1024).transpose(1, 0, 2)
    groups = [[2 * k + c for k in range(8)] for c in range(2)]
    spread = lax.all_to_all(blocks, "dp", split_axis=0, concat_axis=0, tiled=True, axis_index_groups=groups)

    other = lax.ppermute(moved, "tensor", PERM_YL)
    low = tensor < 8
    piece = jnp.concatenate([jnp.where(low, moved, other), jnp.where(low, other, moved)], axis=1)
    feats = ring_gather(piece, tensor % 8)

    squares = lax.psum(jnp.sum(wide * wide, axis=1), "tensor")
    scale = lax.rsqrt(squares / 8192.0 + epsilon)[:, None]

    swapped = [go(w, PERM_C) for w in (w_down, w_gate, tan_up, w_up, tan_gate)]
    first = core == 0
    down = jnp.concatenate(
        [jnp.where(first, w_down, swapped[0]), jnp.where(first, swapped[0], w_down)], axis=1
    )
    weights = [
        jnp.concatenate([mine, theirs], axis=0)
        for mine, theirs in zip((w_gate, tan_up, w_up, tan_gate), swapped[1:])
    ]

    cots = []
    for q, s in ORDER:
        step = jnp.where(first, q, (4 - q) % 4)
        source = (yh ^ s) * 4 + (x ^ step)
        cots.append(lax.dynamic_slice(spread, (source, 0, 0), (1, 128, 1024))[0])
    cots = jnp.concatenate(cots, axis=0)

    back = sum_y_first(cots, down, dot_t)
    gate = sum_x_first(feats, weights[0], dot) * scale
    up_dot = sum_y_first(feats, weights[1], dot) * scale
    up_proj = sum_x_first(feats, weights[2], dot) * scale
    gate_dot = sum_x_first(feats, weights[3], dot) * scale

    sigmoid = jax.nn.sigmoid(gate)
    d1 = sigmoid * (1.0 + gate * (1.0 - sigmoid))
    d2 = sigmoid * (1.0 - sigmoid) * (2.0 + gate * (1.0 - 2.0 * sigmoid))
    gate_adj = (back * (up_dot * d1 + up_proj * d2 * gate_dot) * scale).astype(BF)
    up_adj = (back * d1 * gate_dot * scale).astype(BF)

    outs = []
    for adj in (spread_y_first(gate_adj), spread_x_first(up_adj)):
        theirs = go(dot_0(feats[:, 512:], adj), PERM_C)
        outs.append(dot_0(feats[:, :512], adj) + theirs)
    return tuple(outs)


def solution(mesh):
    return jax.shard_map(
        on_device,
        mesh=mesh,
        in_specs=(
            P("dp", "tensor"),
            P("tensor"),
            P("dp", None),
            P("dp", "tensor"),
            P("dp", "tensor"),
            P("dp", "tensor"),
            P("dp", "tensor"),
            P("tensor", "dp"),
        ),
        out_specs=(P("dp", "tensor"), P("dp", "tensor")),
        check_vma=False,
    )
```

```python
import jax
import jax.numpy as jnp
from jax import lax
from jax.sharding import PartitionSpec as P

epsilon = 1e-05
BF = jnp.bfloat16
F32 = jnp.float32
B = 128

ORDER = ((1, 0), (2, 0), (1, 1), (2, 1), (0, 1), (3, 1), (0, 0), (3, 0))


def split(dp):
    return dp // 8, dp // 2 % 4, dp % 2


def join(yh, x, c):
    return yh * 8 + x * 2 + c


def x_step(q, c):
    return (4 - q) % 4 if c else q


def to_block(q, s):
    pairs = []
    for dp in range(16):
        yh, x, c = split(dp)
        pairs.append((dp, join(yh ^ s, x ^ x_step(q, c), c)))
    return pairs


PERM_P1, PERM_P2, PERM_Y = to_block(1, 0), to_block(3, 0), to_block(0, 1)
PERM_C = [(d, d ^ 1) for d in range(16)]
PERM_YL = [(t, t ^ 8) for t in range(16)]
PERM_UP = [(t, t // 8 * 8 + (t % 8 + 1) % 8) for t in range(16)]
PERM_DOWN = [(t, t // 8 * 8 + (t % 8 + 7) % 8) for t in range(16)]


def transposed():
    pairs = []
    for dp in range(16):
        yh, x, c = split(dp)
        for t in range(16):
            yl, z = t // 8, t % 8
            pairs.append((dp * 16 + t, join(yl, z // 2, c) * 16 + yh * 8 + (z + 2 * x) % 8))
    return pairs


PERM_T = transposed()


def after(value, *earlier):
    return lax.optimization_barrier((value, *earlier))[0]


def dot(a, b):
    return jnp.dot(a, b, preferred_element_type=F32)


def dot_t(a, b):
    return lax.dot_general(a, b, (((1,), (1,)), ((), ())), preferred_element_type=F32)


def dot_0(a, b):
    return lax.dot_general(a, b, (((0,), (0,)), ((), ())), preferred_element_type=F32)


def go(a, perm):
    return lax.ppermute(a, "dp", perm)


def sum_x_first(near, kept):
    far_s = kept[: 2 * B] + near[2 * B :].astype(F32)
    own_s = kept[2 * B :] + near[: 2 * B].astype(F32)
    send = jnp.concatenate([far_s[B:], own_s[B:]], axis=0).astype(BF)
    second = go(send, PERM_P2)
    last = go((far_s[:B] + second[:B].astype(F32)).astype(BF), PERM_Y)
    return own_s[:B] + second[B:].astype(F32) + last.astype(F32), send


def y_send(rows, weight, mul):
    return mul(rows[2 * B : 6 * B], weight).astype(BF)


def sum_y_first(near, rows, weight, mul):
    second = go((mul(rows[: 2 * B], weight) + near[: 2 * B].astype(F32)).astype(BF), PERM_P1)
    kept = mul(rows[6 * B :], weight) + near[2 * B :].astype(F32) + second.astype(F32)
    last = go(kept[B:].astype(BF), PERM_P2)
    return kept[:B] + last.astype(F32)


def spread(first, other):
    first_1, other_1 = lax.optimization_barrier((go(first, PERM_P2), go(other, PERM_Y)))
    first = jnp.concatenate([first, first_1], axis=0)
    pair = jnp.concatenate([other_1, other], axis=0)
    first_2, other_2 = lax.optimization_barrier((go(first, PERM_P1), go(pair, PERM_P2)))
    first = jnp.concatenate([first_2, first], axis=0)
    other = jnp.concatenate([other_1, other_2[:B], pair[B:], other_2[B:]], axis=0)
    first_3, other_3 = go(first, PERM_Y), go(other, PERM_P1)
    return (
        jnp.concatenate([first[: 2 * B], first_3, first[2 * B :]], axis=0),
        jnp.concatenate([other_3[2 * B :], other_3[: 2 * B], other], axis=0),
    )


def on_device(resid, norm_gain, cotangent, w_gate, w_up, tan_gate, tan_up, w_down):
    dp, tensor = lax.axis_index("dp"), lax.axis_index("tensor")
    yh, x, core = dp // 8, dp // 2 % 4, dp % 2
    z = tensor % 8
    hidden = w_gate.shape[1]

    wide = resid.astype(F32)
    squares = jnp.sum(wide * wide, axis=1).reshape(1, B)
    scaled = jnp.concatenate(
        [wide * norm_gain.astype(F32)[None, :], jnp.pad(squares, ((0, 15), (0, 512 - B)))], axis=0
    ).astype(BF)
    moved = lax.ppermute(scaled, ("dp", "tensor"), PERM_T)

    mine = jnp.concatenate([after(w_gate, scaled), w_up, tan_gate], axis=1)
    swapped = go(mine, PERM_C)
    down = jnp.concatenate([w_down, go(w_down, PERM_C)], axis=1)

    other = lax.ppermute(moved, "tensor", PERM_YL)
    low = yh == tensor // 8
    own = jnp.stack([jnp.where(low, moved, other), jnp.where(low, other, moved)])
    cots = {}

    def send_cots(keys, *earlier):
        held = after(cotangent, *earlier)
        for q, s in keys:
            owner = ((yh ^ s) * 4 + (x ^ jnp.where(core == 0, q, (4 - q) % 4))) * 2
            part = jnp.concatenate(
                [lax.dynamic_slice(held, (0, (owner + k) * 512), (B, 512)) for k in (core, 1 - core)], axis=1
            )
            cots[q, s] = part if (q, s) == (0, 0) else go(part, to_block(q, s))

    send_cots(((0, 0), (1, 1), (2, 1), (0, 1), (3, 1)), own)
    parts = [(0, own)]
    up = back_down = own
    for step in range(1, 4):
        up = lax.ppermute(up, "tensor", PERM_UP)
        back_down = lax.ppermute(back_down, "tensor", PERM_DOWN)
        parts += [(-step, up), (step, back_down)]
        if step == 2:
            send_cots(((1, 0), (2, 0), (3, 0)), up, back_down)
    cot_sent = jnp.concatenate([cots[k] for k in ORDER[2:6]], axis=0)
    up, back_down, back_send = lax.optimization_barrier((up, back_down, dot_t(cot_sent, down).astype(BF)))
    cot_rows = jnp.concatenate([cots[k] for k in ORDER], axis=0)
    top = lax.ppermute(up[:1], "tensor", PERM_UP)
    bottom = lax.ppermute(back_down[1:], "tensor", PERM_DOWN)
    parts.append((4, jnp.concatenate([top, bottom], axis=0)))
    gathered = jnp.zeros((2, 2, 4, 144, 512), BF)
    for offset, part in parts:
        place = (z + offset + 8) % 8
        from_x = (place // 2 - x + 4) % 4
        apart = from_x ^ x
        q = jnp.where(core == 0, apart, (4 - apart) % 4)
        half = (place % 2) ^ core
        gathered = lax.dynamic_update_slice(gathered, part[None, :, None], (half, 0, q, 0, 0))
    feats = jnp.concatenate(
        [jnp.concatenate([gathered[h, s, q, :B] for q, s in ORDER], axis=0) for h in range(2)], axis=1
    )
    lengths = gathered[0, :, :, B, :B].astype(F32) + gathered[1, :, :, B, :B].astype(F32)
    lengths = jnp.concatenate([lengths[s, q] for q, s in ORDER], axis=0)
    lengths = jnp.broadcast_to(lengths[:, None], (8 * B, B))

    triple = jnp.concatenate([mine, swapped], axis=0)
    single = jnp.concatenate([tan_up, go(tan_up, PERM_C)], axis=0)

    def products(begin, end, rows, weight):
        return jnp.concatenate([dot(rows[begin:end], weight), lengths[begin:end]], axis=1)

    x_send = products(0, 4 * B, after(feats, cot_rows), triple).astype(BF)
    x_near = go(x_send, PERM_P1)
    back_near = go(after(back_send, x_send), PERM_Y)
    x_kept = products(4 * B, 8 * B, after(feats, x_send), triple)
    up_dot_near = go(y_send(after(feats, back_near, x_kept), single, dot), PERM_Y)
    joint, x_second = sum_x_first(x_near, x_kept)
    back = sum_y_first(back_near, after(cot_rows, x_second), down, dot_t)
    up_dot = sum_y_first(up_dot_near, after(feats, x_second), single, dot)

    scale = lax.rsqrt(joint[:, 3 * hidden : 3 * hidden + 1] / 8192.0 + epsilon)
    joint, up_dot = joint * scale, up_dot * scale
    gate, up_proj, gate_dot = (joint[:, k * hidden : (k + 1) * hidden] for k in range(3))
    sigmoid = jax.nn.sigmoid(gate)
    d1 = sigmoid * (1.0 + gate * (1.0 - sigmoid))
    d2 = sigmoid * (1.0 - sigmoid) * (2.0 + gate * (1.0 - 2.0 * sigmoid))
    gate_adj = (back * (up_dot * d1 + up_proj * d2 * gate_dot) * scale).astype(BF)
    up_adj = (back * d1 * gate_dot * scale).astype(BF)

    first, other = spread(up_adj[:, 256:], jnp.concatenate([gate_adj, up_adj[:, :256]], axis=1))
    rows = (other[:, :hidden], jnp.concatenate([other[:, hidden:], first], axis=1))
    theirs = go(jnp.concatenate([dot_0(feats[:, 512:], adj).astype(BF) for adj in rows], axis=1), PERM_C)
    return tuple(
        dot_0(feats[:, :512], adj) + theirs[:, k * hidden : (k + 1) * hidden].astype(F32)
        for k, adj in enumerate(rows)
    )


def solution(mesh):
    return jax.shard_map(
        on_device,
        mesh=mesh,
        in_specs=(
            P("dp", "tensor"),
            P("tensor"),
            P("dp", None),
            P("dp", "tensor"),
            P("dp", "tensor"),
            P("dp", "tensor"),
            P("dp", "tensor"),
            P("tensor", "dp"),
        ),
        out_specs=(P("dp", "tensor"), P("dp", "tensor")),
        check_vma=False,
    )
```

```python
import jax
import jax.numpy as jnp
from jax import lax
from jax.sharding import PartitionSpec as P

epsilon = 1e-05
BF = jnp.bfloat16
F32 = jnp.float32
B = 128

ORDER = ((1, 0), (2, 0), (1, 1), (2, 1), (0, 1), (3, 1), (0, 0), (3, 0))


def split(dp):
    return dp // 8, dp // 2 % 4, dp % 2


def join(yh, x, c):
    return yh * 8 + x * 2 + c


def x_step(q, c):
    return (4 - q) % 4 if c else q


def to_block(q, s):
    pairs = []
    for dp in range(16):
        yh, x, c = split(dp)
        pairs.append((dp, join(yh ^ s, x ^ x_step(q, c), c)))
    return pairs


PERM_P1, PERM_P2, PERM_Y = to_block(1, 0), to_block(3, 0), to_block(0, 1)
PERM_C = [(d, d ^ 1) for d in range(16)]
PERM_YL = [(t, t ^ 8) for t in range(16)]
PERM_UP = [(t, t // 8 * 8 + (t % 8 + 1) % 8) for t in range(16)]
PERM_DOWN = [(t, t // 8 * 8 + (t % 8 + 7) % 8) for t in range(16)]


def transposed():
    pairs = []
    for dp in range(16):
        yh, x, c = split(dp)
        for t in range(16):
            yl, z = t // 8, t % 8
            pairs.append((dp * 16 + t, join(yl, z // 2, c) * 16 + yh * 8 + (z + 2 * x) % 8))
    return pairs


PERM_T = transposed()


def to_place():
    pairs = []
    for dp in range(16):
        yh, x, c = split(dp)
        for t in range(16):
            q, s = ORDER[t % 8]
            pairs.append((dp * 16 + t, join(yh ^ s, x ^ x_step(q, c), c) * 16 + t))
    return pairs


PERM_W = to_place()


def after(value, *earlier):
    return lax.optimization_barrier((value, *earlier))[0]


def dot(a, b):
    return jnp.dot(a, b, preferred_element_type=F32)


def dot_t(a, b):
    return lax.dot_general(a, b, (((1,), (1,)), ((), ())), preferred_element_type=F32)


def dot_0(a, b):
    return lax.dot_general(a, b, (((0,), (0,)), ((), ())), preferred_element_type=F32)


def go(a, perm):
    return lax.ppermute(a, "dp", perm)


def sum_x_first(near, kept):
    far_s = kept[: 2 * B] + near[2 * B :].astype(F32)
    own_s = kept[2 * B :] + near[: 2 * B].astype(F32)
    send = jnp.concatenate([far_s[B:], own_s[B:]], axis=0).astype(BF)
    second = go(send, PERM_P2)
    third = (far_s[:B] + second[:B].astype(F32)).astype(BF)
    last = go(third, PERM_Y)
    return own_s[:B] + second[B:].astype(F32) + last.astype(F32), send, third


def y_send(rows, weight, mul):
    return mul(rows[2 * B : 6 * B], weight).astype(BF)


def sum_y_first(near, rows, weight, mul):
    second = go((mul(rows[: 2 * B], weight) + near[: 2 * B].astype(F32)).astype(BF), PERM_P1)
    kept = mul(rows[6 * B :], weight) + near[2 * B :].astype(F32) + second.astype(F32)
    last = go(kept[B:].astype(BF), PERM_P2)
    return kept[:B] + last.astype(F32)


def spread(first, middle, other):
    first_1, middle_1, other_1 = lax.optimization_barrier(
        (go(first, PERM_P2), go(middle, PERM_P2), go(other, PERM_Y))
    )
    first = jnp.concatenate([first, first_1], axis=0)
    middle = jnp.concatenate([middle, middle_1], axis=0)
    pair = jnp.concatenate([other_1, other], axis=0)
    first_2, middle_2, other_2 = lax.optimization_barrier(
        (go(first, PERM_P1), go(middle, PERM_Y), go(pair, PERM_P2))
    )
    first = jnp.concatenate([first_2, first], axis=0)
    middle = jnp.concatenate([middle_2, middle], axis=0)
    other = jnp.concatenate([other_1, other_2[:B], pair[B:], other_2[B:]], axis=0)
    first_3, middle_3, other_3 = go(first, PERM_Y), go(middle, PERM_P1), go(other, PERM_P1)
    return (
        jnp.concatenate([first[: 2 * B], first_3, first[2 * B :]], axis=0),
        jnp.concatenate([middle_3[2 * B :], middle_3[: 2 * B], middle], axis=0),
        jnp.concatenate([other_3[2 * B :], other_3[: 2 * B], other], axis=0),
    )


def on_device(resid, norm_gain, cotangent, w_gate, w_up, tan_gate, tan_up, w_down):
    dp, tensor = lax.axis_index("dp"), lax.axis_index("tensor")
    yh, x, core = dp // 8, dp // 2 % 4, dp % 2
    z = tensor % 8
    hidden = w_gate.shape[1]

    wide = resid.astype(F32)
    squares = jnp.sum(wide * wide, axis=1).reshape(1, B)
    scaled = jnp.concatenate(
        [wide * norm_gain.astype(F32)[None, :], jnp.pad(squares, ((0, 15), (0, 512 - B)))], axis=0
    ).astype(BF)
    moved = lax.ppermute(scaled, ("dp", "tensor"), PERM_T)

    mine = jnp.concatenate([after(w_gate, scaled), w_up, tan_gate], axis=1)
    swapped = go(mine, PERM_C)

    other = lax.ppermute(moved, "tensor", PERM_YL)
    same = yh == tensor // 8
    own = jnp.stack([jnp.where(same, moved, other), jnp.where(same, other, moved)])
    tan_up, w_down = after(tan_up, scaled), after(w_down, scaled)
    single = jnp.concatenate([tan_up, go(tan_up, PERM_C)], axis=0)
    down = jnp.concatenate([w_down, go(w_down, PERM_C)], axis=1)

    to_q = jnp.array([q for q, _ in ORDER])[z]
    to_s = jnp.array([s for _, s in ORDER])[z]
    owner = ((yh ^ to_s) * 4 + (x ^ jnp.where(core == 0, to_q, (4 - to_q) % 4))) * 2
    held = after(cotangent, own)
    cot_piece = jnp.concatenate(
        [lax.dynamic_slice(held, (0, (owner + k) * 512), (B, 512)) for k in (core, 1 - core)], axis=1
    )
    cot_piece = lax.ppermute(cot_piece, ("dp", "tensor"), PERM_W)

    parts = [(0, own)]
    up = low = own
    for step in range(1, 4):
        up = lax.ppermute(up, "tensor", PERM_UP)
        low = lax.ppermute(low, "tensor", PERM_DOWN)
        parts += [(-step, up), (step, low)]
        if step == 2:
            up, low, cot_piece = lax.optimization_barrier((up, low, cot_piece))
    up, low, single, down = lax.optimization_barrier((up, low, single, down))
    top = lax.ppermute(up[:1], "tensor", PERM_UP)
    bottom = lax.ppermute(low[1:], "tensor", PERM_DOWN)
    parts.append((4, jnp.concatenate([top, bottom], axis=0)))
    gathered = jnp.zeros((2, 2, 4, 144, 512), BF)
    for offset, part in parts:
        place = (z + offset + 8) % 8
        from_x = (place // 2 - x + 4) % 4
        apart = from_x ^ x
        q = jnp.where(core == 0, apart, (4 - apart) % 4)
        half = (place % 2) ^ core
        gathered = lax.dynamic_update_slice(gathered, part[None, :, None], (half, 0, q, 0, 0))
    feats = jnp.concatenate(
        [jnp.concatenate([gathered[h, s, q, :B] for q, s in ORDER], axis=0) for h in range(2)], axis=1
    )
    lengths = gathered[0, :, :, B, :B].astype(F32) + gathered[1, :, :, B, :B].astype(F32)
    lengths = jnp.concatenate([lengths[s, q] for q, s in ORDER], axis=0)
    lengths = jnp.broadcast_to(lengths[:, None], (8 * B, B))

    triple = jnp.concatenate([mine, swapped], axis=0)

    def products(begin, end, rows, weight):
        return jnp.concatenate([dot(rows[begin:end], weight), lengths[begin:end]], axis=1)

    x_send = products(0, 4 * B, feats, triple).astype(BF)
    x_near = go(x_send, PERM_P1)
    up_dot_near = go(y_send(after(feats, x_send), single, dot), PERM_Y)

    cot_rows = jnp.zeros((8 * B, 1024), BF)
    up = down_part = own = after(cot_piece, x_send)
    parts = [(0, own)]
    for step in range(1, 4):
        up = lax.ppermute(up, "tensor", PERM_UP)
        down_part = lax.ppermute(down_part, "tensor", PERM_DOWN)
        parts += [(-step, up), (step, down_part)]
        if step == 2:
            x_kept = products(4 * B, 8 * B, after(feats, up, down_part), triple)
    x_near = after(x_near, up, down_part)
    top = lax.ppermute(up[:64], "tensor", PERM_UP)
    bottom = lax.ppermute(down_part[64:], "tensor", PERM_DOWN)
    parts.append((4, jnp.concatenate([top, bottom], axis=0)))
    for offset, part in parts:
        cot_rows = lax.dynamic_update_slice(cot_rows, part, ((z + offset + 8) % 8 * B, 0))

    back_send = y_send(cot_rows, down, dot_t)
    back_near = go(back_send, PERM_Y)
    joint, x_second, x_third = sum_x_first(x_near, x_kept)
    up_dot = sum_y_first(up_dot_near, after(feats, x_second), single, dot)
    back = sum_y_first(back_near, after(cot_rows, x_second), down, dot_t)

    scale = lax.rsqrt(joint[:, 3 * hidden : 3 * hidden + 1] / 8192.0 + epsilon)
    joint, up_dot = joint * scale, up_dot * scale
    gate, up_proj, gate_dot = (joint[:, k * hidden : (k + 1) * hidden] for k in range(3))
    sigmoid = jax.nn.sigmoid(gate)
    d1 = sigmoid * (1.0 + gate * (1.0 - sigmoid))
    d2 = sigmoid * (1.0 - sigmoid) * (2.0 + gate * (1.0 - 2.0 * sigmoid))
    gate_adj = (back * (up_dot * d1 + up_proj * d2 * gate_dot) * scale).astype(BF)
    up_adj = (back * d1 * gate_dot * scale).astype(BF)

    first, middle, other = spread(
        up_adj[:, 256:], jnp.concatenate([gate_adj[:, 512:], up_adj[:, :256]], axis=1), gate_adj[:, :512]
    )
    rows = (
        jnp.concatenate([other, middle[:, : hidden - 512]], axis=1),
        jnp.concatenate([middle[:, hidden - 512 :], first], axis=1),
    )
    theirs = go(jnp.concatenate([dot_0(feats[:, 512:], adj).astype(BF) for adj in rows], axis=1), PERM_C)
    sums = lax.optimization_barrier([dot_0(feats[:, :512], adj) for adj in rows])
    return tuple(
        part + theirs[:, k * hidden : (k + 1) * hidden].astype(F32) for k, part in enumerate(sums)
    )


def solution(mesh):
    return jax.shard_map(
        on_device,
        mesh=mesh,
        in_specs=(
            P("dp", "tensor"),
            P("tensor"),
            P("dp", None),
            P("dp", "tensor"),
            P("dp", "tensor"),
            P("dp", "tensor"),
            P("dp", "tensor"),
            P("tensor", "dp"),
        ),
        out_specs=(P("dp", "tensor"), P("dp", "tensor")),
        check_vma=False,
    )
```

```python
import jax
import jax.numpy as jnp
from jax import lax
from jax.sharding import PartitionSpec as P

epsilon = 1e-05
BF = jnp.bfloat16
F32 = jnp.float32
B = 128

ORDER = ((1, 0), (2, 0), (1, 1), (2, 1), (0, 1), (3, 1), (0, 0), (3, 0))


def split(dp):
    return dp // 8, dp // 2 % 4, dp % 2


def join(yh, x, c):
    return yh * 8 + x * 2 + c


def x_step(q, c):
    return (4 - q) % 4 if c else q


def to_block(q, s):
    pairs = []
    for dp in range(16):
        yh, x, c = split(dp)
        pairs.append((dp, join(yh ^ s, x ^ x_step(q, c), c)))
    return pairs


PERM_P1, PERM_P2, PERM_Y = to_block(1, 0), to_block(3, 0), to_block(0, 1)
PERM_C = [(d, d ^ 1) for d in range(16)]
PERM_YL = [(t, t ^ 8) for t in range(16)]
PERM_UP = [(t, t // 8 * 8 + (t % 8 + 1) % 8) for t in range(16)]
PERM_DOWN = [(t, t // 8 * 8 + (t % 8 + 7) % 8) for t in range(16)]


def transposed():
    pairs = []
    for dp in range(16):
        yh, x, c = split(dp)
        for t in range(16):
            yl, z = t // 8, t % 8
            pairs.append((dp * 16 + t, join(yl, z // 2, c) * 16 + yh * 8 + (z + 2 * x) % 8))
    return pairs


PERM_T = transposed()


def to_place():
    pairs = []
    for dp in range(16):
        yh, x, c = split(dp)
        for t in range(16):
            q, s = ORDER[t % 8]
            pairs.append((dp * 16 + t, join(yh ^ s, x ^ x_step(q, c), c) * 16 + t))
    return pairs


PERM_W = to_place()


def after(value, *earlier):
    return lax.optimization_barrier((value, *earlier))[0]


def dot(a, b):
    return jnp.dot(a, b, preferred_element_type=F32)


def dot_t(a, b):
    return lax.dot_general(a, b, (((1,), (1,)), ((), ())), preferred_element_type=F32)


def dot_0(a, b):
    return lax.dot_general(a, b, (((0,), (0,)), ((), ())), preferred_element_type=F32)


def go(a, perm):
    return lax.ppermute(a, "dp", perm)


def sum_x_first(near, kept):
    far_s = kept[: 2 * B] + near[2 * B :].astype(F32)
    own_s = kept[2 * B :] + near[: 2 * B].astype(F32)
    send = jnp.concatenate([far_s[B:], own_s[B:]], axis=0).astype(BF)
    second = go(send, PERM_P2)
    third = (far_s[:B] + second[:B].astype(F32)).astype(BF)
    last = go(third, PERM_Y)
    return own_s[:B] + second[B:].astype(F32) + last.astype(F32), send, third


def sum_x_y_x(near, kept):
    away = (kept[: 2 * B] + near[2 * B :].astype(F32)).astype(BF)
    second = go(away, PERM_Y)
    own_s = kept[2 * B :] + near[: 2 * B].astype(F32) + second.astype(F32)
    last = go(own_s[B:].astype(BF), PERM_P2)
    return own_s[:B] + last.astype(F32)


def y_send(rows, weight, mul):
    return mul(rows[2 * B : 6 * B], weight).astype(BF)


def sum_y_first(near, rows, weight, mul):
    second = go((mul(rows[: 2 * B], weight) + near[: 2 * B].astype(F32)).astype(BF), PERM_P1)
    kept = mul(rows[6 * B :], weight) + near[2 * B :].astype(F32) + second.astype(F32)
    last = go(kept[B:].astype(BF), PERM_P2)
    return kept[:B] + last.astype(F32)


def spread(first, middle, other):
    first_1, middle_1, other_1 = lax.optimization_barrier(
        (go(first, PERM_P2), go(middle, PERM_P2), go(other, PERM_Y))
    )
    first = jnp.concatenate([first, first_1], axis=0)
    middle = jnp.concatenate([middle, middle_1], axis=0)
    pair = jnp.concatenate([other_1, other], axis=0)
    first_2, middle_2, other_2 = lax.optimization_barrier(
        (go(first, PERM_P1), go(middle, PERM_Y), go(pair, PERM_P2))
    )
    first = jnp.concatenate([first_2, first], axis=0)
    middle = jnp.concatenate([middle_2, middle], axis=0)
    other = jnp.concatenate([other_1, other_2[:B], pair[B:], other_2[B:]], axis=0)
    first_3, middle_3, other_3 = go(first, PERM_Y), go(middle, PERM_P1), go(other, PERM_P1)
    return (
        jnp.concatenate([first[: 2 * B], first_3, first[2 * B :]], axis=0),
        jnp.concatenate([middle_3[2 * B :], middle_3[: 2 * B], middle], axis=0),
        jnp.concatenate([other_3[2 * B :], other_3[: 2 * B], other], axis=0),
    )


def on_device(resid, norm_gain, cotangent, w_gate, w_up, tan_gate, tan_up, w_down):
    dp, tensor = lax.axis_index("dp"), lax.axis_index("tensor")
    yh, x, core = dp // 8, dp // 2 % 4, dp % 2
    z = tensor % 8
    hidden = w_gate.shape[1]

    wide = resid.astype(F32)
    squares = jnp.sum(wide * wide, axis=1).reshape(1, B)
    scaled = jnp.concatenate(
        [wide * norm_gain.astype(F32)[None, :], jnp.pad(squares, ((0, 15), (0, 512 - B)))], axis=0
    ).astype(BF)
    moved = lax.ppermute(scaled, ("dp", "tensor"), PERM_T)

    mine = jnp.concatenate([after(w_gate, scaled), w_up, tan_gate], axis=1)
    swapped = go(mine, PERM_C)

    other = lax.ppermute(moved, "tensor", PERM_YL)
    same = yh == tensor // 8
    own = jnp.stack([jnp.where(same, moved, other), jnp.where(same, other, moved)])
    tan_up, w_down = after(tan_up, scaled), after(w_down, scaled)
    single = jnp.concatenate([tan_up, go(tan_up, PERM_C)], axis=0)
    down = jnp.concatenate([w_down, go(w_down, PERM_C)], axis=1)

    to_q = jnp.array([q for q, _ in ORDER])[z]
    to_s = jnp.array([s for _, s in ORDER])[z]
    owner = ((yh ^ to_s) * 4 + (x ^ jnp.where(core == 0, to_q, (4 - to_q) % 4))) * 2
    held = after(cotangent, own)
    cot_piece = jnp.concatenate(
        [lax.dynamic_slice(held, (0, (owner + k) * 512), (B, 512)) for k in (core, 1 - core)], axis=1
    )
    cot_piece = lax.ppermute(cot_piece, ("dp", "tensor"), PERM_W)

    parts = [(0, own)]
    up = low = own
    for step in range(1, 4):
        up = lax.ppermute(up, "tensor", PERM_UP)
        low = lax.ppermute(low, "tensor", PERM_DOWN)
        parts += [(-step, up), (step, low)]
        if step == 2:
            up, low, cot_piece = lax.optimization_barrier((up, low, cot_piece))
    up, low, single, down = lax.optimization_barrier((up, low, single, down))
    top = lax.ppermute(up[:1], "tensor", PERM_UP)
    bottom = lax.ppermute(low[1:], "tensor", PERM_DOWN)
    parts.append((4, jnp.concatenate([top, bottom], axis=0)))
    gathered = jnp.zeros((2, 2, 4, 144, 512), BF)
    for offset, part in parts:
        place = (z + offset + 8) % 8
        from_x = (place // 2 - x + 4) % 4
        apart = from_x ^ x
        q = jnp.where(core == 0, apart, (4 - apart) % 4)
        half = (place % 2) ^ core
        gathered = lax.dynamic_update_slice(gathered, part[None, :, None], (half, 0, q, 0, 0))
    feats = jnp.concatenate(
        [jnp.concatenate([gathered[h, s, q, :B] for q, s in ORDER], axis=0) for h in range(2)], axis=1
    )
    lengths = gathered[0, :, :, B, :B].astype(F32) + gathered[1, :, :, B, :B].astype(F32)
    lengths = jnp.concatenate([lengths[s, q] for q, s in ORDER], axis=0)
    lengths = jnp.broadcast_to(lengths[:, None], (8 * B, B))

    triple = jnp.concatenate([mine, swapped], axis=0)

    def products(begin, end, rows, weight):
        return jnp.concatenate([dot(rows[begin:end], weight), lengths[begin:end]], axis=1)

    double, third_weight = triple[:, : 2 * hidden], triple[:, 2 * hidden :]
    m_send = dot(feats[: 4 * B], third_weight).astype(BF)
    m_near = go(m_send, PERM_P1)
    x_send = products(0, 4 * B, after(feats, m_send), double).astype(BF)
    x_near = go(x_send, PERM_P1)
    up_dot_near = go(y_send(after(feats, x_send), single, dot), PERM_Y)

    cot_rows = jnp.zeros((8 * B, 1024), BF)
    up = down_part = own = after(cot_piece, x_send)
    parts = [(0, own)]
    for step in range(1, 4):
        up = lax.ppermute(up, "tensor", PERM_UP)
        down_part = lax.ppermute(down_part, "tensor", PERM_DOWN)
        parts += [(-step, up), (step, down_part)]
        if step == 1:
            m_kept = dot(after(feats, up, down_part)[4 * B :], third_weight)
        if step == 2:
            x_kept = products(4 * B, 8 * B, after(feats, up, down_part), double)
            m_near = after(m_near, up, down_part)
    x_near = after(x_near, up, down_part)
    top = lax.ppermute(up[:64], "tensor", PERM_UP)
    bottom = lax.ppermute(down_part[64:], "tensor", PERM_DOWN)
    parts.append((4, jnp.concatenate([top, bottom], axis=0)))
    for offset, part in parts:
        cot_rows = lax.dynamic_update_slice(cot_rows, part, ((z + offset + 8) % 8 * B, 0))

    back_send = y_send(cot_rows, down, dot_t)
    back_near = go(back_send, PERM_Y)
    gate_dot = sum_x_y_x(m_near, m_kept)
    joint, x_second, x_third = sum_x_first(x_near, x_kept)
    up_dot = sum_y_first(up_dot_near, after(feats, back_send), single, dot)
    back = sum_y_first(back_near, after(cot_rows, x_second), down, dot_t)

    scale = lax.rsqrt(joint[:, 2 * hidden : 2 * hidden + 1] / 8192.0 + epsilon)
    joint, up_dot, gate_dot = joint * scale, up_dot * scale, gate_dot * scale
    gate, up_proj = joint[:, :hidden], joint[:, hidden : 2 * hidden]
    sigmoid = jax.nn.sigmoid(gate)
    d1 = sigmoid * (1.0 + gate * (1.0 - sigmoid))
    d2 = sigmoid * (1.0 - sigmoid) * (2.0 + gate * (1.0 - 2.0 * sigmoid))
    gate_adj = (back * (up_dot * d1 + up_proj * d2 * gate_dot) * scale).astype(BF)
    up_adj = (back * d1 * gate_dot * scale).astype(BF)

    first, middle, other = spread(
        up_adj[:, 256:], jnp.concatenate([gate_adj[:, 512:], up_adj[:, :256]], axis=1), gate_adj[:, :512]
    )
    rows = (
        jnp.concatenate([other, middle[:, : hidden - 512]], axis=1),
        jnp.concatenate([middle[:, hidden - 512 :], first], axis=1),
    )
    theirs = go(jnp.concatenate([dot_0(feats[:, 512:], adj).astype(BF) for adj in rows], axis=1), PERM_C)
    sums = lax.optimization_barrier([dot_0(feats[:, :512], adj) for adj in rows])
    return tuple(
        part + theirs[:, k * hidden : (k + 1) * hidden].astype(F32) for k, part in enumerate(sums)
    )


def solution(mesh):
    return jax.shard_map(
        on_device,
        mesh=mesh,
        in_specs=(
            P("dp", "tensor"),
            P("tensor"),
            P("dp", None),
            P("dp", "tensor"),
            P("dp", "tensor"),
            P("dp", "tensor"),
            P("dp", "tensor"),
            P("tensor", "dp"),
        ),
        out_specs=(P("dp", "tensor"), P("dp", "tensor")),
        check_vma=False,
    )
```

```python
import jax
import jax.numpy as jnp
from jax import lax
from jax.sharding import PartitionSpec as P

epsilon = 1e-05
BF = jnp.bfloat16
F32 = jnp.float32
B = 128

ORDER = ((1, 0), (2, 0), (1, 1), (2, 1), (0, 1), (3, 1), (0, 0), (3, 0))


def split(dp):
    return dp // 8, dp // 2 % 4, dp % 2


def join(yh, x, c):
    return yh * 8 + x * 2 + c


def x_step(q, c):
    return (4 - q) % 4 if c else q


def to_block(q, s):
    pairs = []
    for dp in range(16):
        yh, x, c = split(dp)
        pairs.append((dp, join(yh ^ s, x ^ x_step(q, c), c)))
    return pairs


PERM_P1, PERM_P2, PERM_Y = to_block(1, 0), to_block(3, 0), to_block(0, 1)
PERM_C = [(d, d ^ 1) for d in range(16)]
PERM_YL = [(t, t ^ 8) for t in range(16)]
PERM_UP = [(t, t // 8 * 8 + (t % 8 + 1) % 8) for t in range(16)]
PERM_DOWN = [(t, t // 8 * 8 + (t % 8 + 7) % 8) for t in range(16)]


def transposed():
    pairs = []
    for dp in range(16):
        yh, x, c = split(dp)
        for t in range(16):
            yl, z = t // 8, t % 8
            pairs.append((dp * 16 + t, join(yl, z // 2, c) * 16 + yh * 8 + (z + 2 * x) % 8))
    return pairs


PERM_T = transposed()


def to_place():
    pairs = []
    for dp in range(16):
        yh, x, c = split(dp)
        for t in range(16):
            q, s = ORDER[t % 8]
            pairs.append((dp * 16 + t, join(yh ^ s, x ^ x_step(q, c), c) * 16 + t))
    return pairs


PERM_W = to_place()


def after(value, *earlier):
    return lax.optimization_barrier((value, *earlier))[0]


def dot(a, b):
    return jnp.dot(a, b, preferred_element_type=F32)


def dot_t(a, b):
    return lax.dot_general(a, b, (((1,), (1,)), ((), ())), preferred_element_type=F32)


def dot_0(a, b):
    return lax.dot_general(a, b, (((0,), (0,)), ((), ())), preferred_element_type=F32)


def go(a, perm):
    return lax.ppermute(a, "dp", perm)


def sum_x_first(near, kept):
    far_s = kept[: 2 * B] + near[2 * B :].astype(F32)
    own_s = kept[2 * B :] + near[: 2 * B].astype(F32)
    send = jnp.concatenate([far_s[B:], own_s[B:]], axis=0).astype(BF)
    second = go(send, PERM_P2)
    third = (far_s[:B] + second[:B].astype(F32)).astype(BF)
    last = go(third, PERM_Y)
    return own_s[:B] + second[B:].astype(F32) + last.astype(F32), send, third


def sum_x_y_x(near, kept):
    away = (kept[: 2 * B] + near[2 * B :].astype(F32)).astype(BF)
    second = go(away, PERM_Y)
    own_s = kept[2 * B :] + near[: 2 * B].astype(F32) + second.astype(F32)
    last = go(own_s[B:].astype(BF), PERM_P2)
    return own_s[:B] + last.astype(F32)


def y_send(rows, weight, mul):
    return mul(rows[2 * B : 6 * B], weight).astype(BF)


def sum_y_first(near, rows, weight, mul):
    second = go((mul(rows[: 2 * B], weight) + near[: 2 * B].astype(F32)).astype(BF), PERM_P1)
    kept = mul(rows[6 * B :], weight) + near[2 * B :].astype(F32) + second.astype(F32)
    last = go(kept[B:].astype(BF), PERM_P2)
    return kept[:B] + last.astype(F32)


def spread(first, middle, other):
    first_1, middle_1, other_1 = lax.optimization_barrier(
        (go(first, PERM_P2), go(middle, PERM_P2), go(other, PERM_Y))
    )
    first = jnp.concatenate([first, first_1], axis=0)
    middle = jnp.concatenate([middle, middle_1], axis=0)
    pair = jnp.concatenate([other_1, other], axis=0)
    first_2, middle_2, other_2 = lax.optimization_barrier(
        (go(first, PERM_P1), go(middle, PERM_Y), go(pair, PERM_P2))
    )
    first = jnp.concatenate([first_2, first], axis=0)
    middle = jnp.concatenate([middle_2, middle], axis=0)
    other = jnp.concatenate([other_1, other_2[:B], pair[B:], other_2[B:]], axis=0)
    first_3, middle_3, other_3 = go(first, PERM_Y), go(middle, PERM_P1), go(other, PERM_P1)
    return (
        jnp.concatenate([first[: 2 * B], first_3, first[2 * B :]], axis=0),
        jnp.concatenate([middle_3[2 * B :], middle_3[: 2 * B], middle], axis=0),
        jnp.concatenate([other_3[2 * B :], other_3[: 2 * B], other], axis=0),
    )


def on_device(resid, norm_gain, cotangent, w_gate, w_up, tan_gate, tan_up, w_down):
    dp, tensor = lax.axis_index("dp"), lax.axis_index("tensor")
    yh, x, core = dp // 8, dp // 2 % 4, dp % 2
    z = tensor % 8
    hidden = w_gate.shape[1]

    wide = resid.astype(F32)
    squares = jnp.sum(wide * wide, axis=1).reshape(1, B)
    scaled = jnp.concatenate(
        [wide * norm_gain.astype(F32)[None, :], jnp.pad(squares, ((0, 15), (0, 512 - B)))], axis=0
    ).astype(BF)
    moved = lax.ppermute(scaled, ("dp", "tensor"), PERM_T)

    mine = jnp.concatenate([after(w_gate, scaled), w_up, tan_gate], axis=1)
    swapped = go(mine, PERM_C)

    other = lax.ppermute(moved, "tensor", PERM_YL)
    same = yh == tensor // 8
    own = jnp.stack([jnp.where(same, moved, other), jnp.where(same, other, moved)])
    tan_up, w_down = after(tan_up, scaled), after(w_down, scaled)
    single = jnp.concatenate([tan_up, go(tan_up, PERM_C)], axis=0)
    down = jnp.concatenate([w_down, go(w_down, PERM_C)], axis=1)

    to_q = jnp.array([q for q, _ in ORDER])[z]
    to_s = jnp.array([s for _, s in ORDER])[z]
    owner = ((yh ^ to_s) * 4 + (x ^ jnp.where(core == 0, to_q, (4 - to_q) % 4))) * 2
    held = after(cotangent, own)
    cot_piece = jnp.concatenate(
        [lax.dynamic_slice(held, (0, (owner + k) * 512), (B, 512)) for k in (core, 1 - core)], axis=1
    )
    cot_piece = lax.ppermute(cot_piece, ("dp", "tensor"), PERM_W)

    parts = [(0, own)]
    up = low = own
    for step in range(1, 4):
        up = lax.ppermute(up, "tensor", PERM_UP)
        low = lax.ppermute(low, "tensor", PERM_DOWN)
        parts += [(-step, up), (step, low)]
        if step == 2:
            up, low, cot_piece = lax.optimization_barrier((up, low, cot_piece))
    up, low, single, down = lax.optimization_barrier((up, low, single, down))
    top = lax.ppermute(up[:1], "tensor", PERM_UP)
    bottom = lax.ppermute(low[1:], "tensor", PERM_DOWN)
    parts.append((4, jnp.concatenate([top, bottom], axis=0)))
    gathered = jnp.zeros((2, 2, 4, 144, 512), BF)
    for offset, part in parts:
        place = (z + offset + 8) % 8
        from_x = (place // 2 - x + 4) % 4
        apart = from_x ^ x
        q = jnp.where(core == 0, apart, (4 - apart) % 4)
        half = (place % 2) ^ core
        gathered = lax.dynamic_update_slice(gathered, part[None, :, None], (half, 0, q, 0, 0))
    feats = jnp.concatenate(
        [jnp.concatenate([gathered[h, s, q, :B] for q, s in ORDER], axis=0) for h in range(2)], axis=1
    )
    lengths = gathered[0, :, :, B, :B].astype(F32) + gathered[1, :, :, B, :B].astype(F32)
    lengths = jnp.concatenate([lengths[s, q] for q, s in ORDER], axis=0)
    lengths = jnp.broadcast_to(lengths[:, None], (8 * B, B))

    triple = jnp.concatenate([mine, swapped], axis=0)

    def products(begin, end, rows, weight):
        return jnp.concatenate([dot(rows[begin:end], weight), lengths[begin:end]], axis=1)

    double, third_weight = triple[:, : 2 * hidden], triple[:, 2 * hidden :]
    m_send = dot(feats[: 4 * B], third_weight).astype(BF)
    m_near = go(m_send, PERM_P1)
    x_send = products(0, 4 * B, after(feats, m_send), double).astype(BF)
    x_near = go(x_send, PERM_P1)
    up_dot_near = go(y_send(after(feats, x_send), single, dot), PERM_Y)

    cot_rows = jnp.zeros((8 * B, 1024), BF)
    up = down_part = own = after(cot_piece, x_send)
    parts = [(0, own)]
    for step in range(1, 4):
        up = lax.ppermute(up, "tensor", PERM_UP)
        down_part = lax.ppermute(down_part, "tensor", PERM_DOWN)
        parts += [(-step, up), (step, down_part)]
        if step == 1:
            m_kept = dot(after(feats, up, down_part)[4 * B :], third_weight)
        if step == 2:
            x_kept = products(4 * B, 8 * B, after(feats, up, down_part), double)
            m_near = after(m_near, up, down_part)
    x_near = after(x_near, up, down_part)
    top = lax.ppermute(up[:64], "tensor", PERM_UP)
    bottom = lax.ppermute(down_part[64:], "tensor", PERM_DOWN)
    parts.append((4, jnp.concatenate([top, bottom], axis=0)))
    for offset, part in parts:
        cot_rows = lax.dynamic_update_slice(cot_rows, part, ((z + offset + 8) % 8 * B, 0))

    back_send = y_send(cot_rows, down, dot_t)
    back_near = go(back_send, PERM_Y)
    gate_dot = sum_x_y_x(m_near, m_kept)
    joint, x_second, x_third = sum_x_first(x_near, x_kept)
    up_dot = sum_y_first(up_dot_near, after(feats, back_send), single, dot)
    back = sum_y_first(back_near, after(cot_rows, x_second), down, dot_t)

    scale = lax.rsqrt(joint[:, 2 * hidden : 2 * hidden + 1] / 8192.0 + epsilon)
    joint, up_dot, gate_dot = joint * scale, up_dot * scale, gate_dot * scale
    gate, up_proj = joint[:, :hidden], joint[:, hidden : 2 * hidden]
    sigmoid = jax.nn.sigmoid(gate)
    d1 = sigmoid * (1.0 + gate * (1.0 - sigmoid))
    d2 = sigmoid * (1.0 - sigmoid) * (2.0 + gate * (1.0 - 2.0 * sigmoid))
    gate_adj = (back * (up_dot * d1 + up_proj * d2 * gate_dot) * scale).astype(BF)
    up_adj = (back * d1 * gate_dot * scale).astype(BF)

    first, middle, other = spread(
        up_adj[:, 256:], jnp.concatenate([gate_adj[:, 512:], up_adj[:, :256]], axis=1), gate_adj[:, :512]
    )
    rows = (
        jnp.concatenate([other, middle[:, : hidden - 512]], axis=1),
        jnp.concatenate([middle[:, hidden - 512 :], first], axis=1),
    )
    theirs = [go(dot_0(feats[:, 512:], adj).astype(BF), PERM_C) for adj in rows]
    sums = lax.optimization_barrier([dot_0(feats[:, :512], adj) for adj in rows])
    return tuple(own + part.astype(F32) for own, part in zip(sums, theirs))


def solution(mesh):
    return jax.shard_map(
        on_device,
        mesh=mesh,
        in_specs=(
            P("dp", "tensor"),
            P("tensor"),
            P("dp", None),
            P("dp", "tensor"),
            P("dp", "tensor"),
            P("dp", "tensor"),
            P("dp", "tensor"),
            P("tensor", "dp"),
        ),
        out_specs=(P("dp", "tensor"), P("dp", "tensor")),
        check_vma=False,
    )
```
